32 devices in a mesh: sky: 8 (over y, x, core), gz: 4 (over z).
Axes of the slice: x: 2, y: 2, z: 4, core: 2. Of those that a mesh axis runs over, the one named last changes fastest.
Arguments:
- spectra: bfloat16 [2048, 1032], P('sky', 'gz'), may hold values from -6 to 6
- kernel: bfloat16 [2048, 16], P('sky'), may hold values from 0.049804688 to 0.59765625
- owner: int32 [2048, 1], P('sky'), may hold values from 0 to 7; in each aligned block of 256 rows (0 to 255, 256 to 511, ...) at most 40 rows name the same one
- offset: int32 [2048], P('sky'), may hold values from 0 to 8191
Outputs:
- spectrum: float32 [2, 256, 256, 1032], P(None, None, ('sky', 'gz'))
The draws below stay inside these ranges and needn't reach their ends.
Inputs may be any that keep to these rules, and one draw needn't show every extreme that they name: `owner`: in each aligned block of 256 rows no sky index is named by more than 40 rows, a bound that some block reaches.
All inputs are finite; a program needn't handle non-finite values.
Results may differ from the reference program's by a relative error of at most 0.0063.
Values may be sent and summed in bfloat16 or wider, within the bound.
A program may use at most 128 MiB of HBM per device.

```python
import math
import jax
import jax.numpy as jnp
import numpy as np

NX = 256
NY = 256
NW = 1032
KSIDE = 4
FIB_DEV = 256
FIBRES = 2048
N_SKY = 8


def set_ends(array, rng, smallest, largest):
    shape = array.shape
    spot = [jax.random.randint(jax.random.fold_in(rng, axis), (), 0, shape[axis]) for axis in range(len(shape))]
    array = array.at[tuple(spot)].set(smallest)
    longest = shape.index(max(shape))
    spot[longest] = (spot[longest] + 1) % shape[longest]
    return array.at[tuple(spot)].set(largest)


def level_of(key, shape, shards, low, largest):
    gain = 1.0
    for axis_at, blocks in shards:
        draws = jax.random.uniform(jax.random.fold_in(jax.random.fold_in(key, 6), axis_at), (blocks,), jnp.float32, low / len(shards), largest / len(shards))
        gain = gain * jnp.repeat(jnp.exp(draws), shape[axis_at] // blocks).reshape((-1,) + (1,) * (len(shape) - 1 - axis_at))
    return gain


def shared_out(stream_key, own, number, rows, count, top, most, skew):
    order = jax.random.permutation(stream_key, count)
    heavy_load, ordinary = load_shares(count, rows * top, most, skew, True), load_shares(count, rows * top, most, skew, False)
    places = jnp.arange(count)

    def named(tallies, rotation):
        used = int((tallies > 0).sum())
        fixed = max(1, used // 4)
        moved = fixed + (places - fixed + rotation * (used - fixed)) % max(1, count - fixed)
        return jnp.zeros((count,), jnp.int32).at[order[jnp.where(places < fixed, places, moved)]].set(jnp.asarray(tallies, jnp.int32))

    tallies = jnp.where(number % 4 == 0, named(heavy_load, number // 4), named(ordinary, number - number // 4 - 1))
    mixed = jax.random.permutation(jax.random.fold_in(own, 3), count)
    source_of, sink = mixed[0:count // 2 * 2:2], mixed[1:count // 2 * 2:2]
    room = jnp.minimum(tallies[source_of] - 1, most - tallies[sink]) // 2
    room = jnp.where((source_of == order[0]) | (sink == order[0]) | (tallies[sink] == 0), 0, jnp.maximum(room, 0))
    moved = jax.random.randint(jax.random.fold_in(own, 4), (count // 2,), 0, 1 << 20) % (room + 1)
    tallies = tallies.at[source_of].add(-moved).at[sink].add(moved)
    members = jnp.searchsorted(jnp.cumsum(tallies), jnp.arange(rows * top), side="right").astype(jnp.int32)
    grid = members.reshape(top, rows).T
    grid = grid[jax.random.permutation(jax.random.fold_in(own, 1), rows)]
    rotation = jax.random.randint(jax.random.fold_in(own, 2), (rows, 1), 0, top)
    return jnp.take_along_axis(grid, (jnp.arange(top)[None, :] + rotation) % top, axis=1)


def load_shares(count, total, bound, lean, full):
    portions = [(1 << 20) // math.isqrt(rank ** lean) + 1 for rank in range(1, count + 1)]
    largest = bound if full else min(bound, max(-(-total // count), total * portions[0] // sum(portions)))
    least = 1 if total - largest >= count - 1 else 0
    given, surplus = [largest] + [least] * (count - 1), total - largest - least * (count - 1)
    while surplus > 0:
        candidates = [i for i in range(1, count) if given[i] < largest] or [i for i in range(1, count) if given[i] < bound]
        pool, budget = sum([portions[i] for i in candidates]), surplus
        for i in candidates:
            more = min(bound - given[i], max(1, budget * portions[i] // pool), surplus)
            given[i] = given[i] + more
            surplus = surplus - more
    return np.array(given)


def normal_values(stream_key, dims, scale, reach, pieces=(), held_as=jnp.bfloat16):
    level = level_of(stream_key, dims, pieces, -0.22, 0.18) if pieces else 1.0
    drawn = jax.random.normal(stream_key, dims, jnp.float32) * scale * level
    return jnp.minimum(jnp.maximum(drawn, -reach), reach).astype(held_as)


def setup_inputs(seed: int = 0) -> dict:
    arg_keys = jax.random.split(jax.random.key(seed), 5)
    spectra = normal_values(arg_keys[0], (FIBRES, NW), 1.0, 6.0, ((0, 8), (1, 4)))
    kernel = jnp.clip(0.049804688 + 0.54785156 * jax.random.uniform(arg_keys[1], (FIBRES, KSIDE * KSIDE), jnp.float32) ** level_of(arg_keys[1], (FIBRES, KSIDE * KSIDE), ((0, 8),), -0.2, 0.2), 0.049804688, 0.59765625).astype(jnp.bfloat16)
    owner_keys = jax.random.split(jax.random.fold_in(arg_keys[2], 1), FIBRES // FIB_DEV)
    owner_turns = jax.random.permutation(jax.random.fold_in(arg_keys[2], 3), FIBRES // FIB_DEV)
    owner = jax.vmap(lambda own, number: shared_out(jax.random.fold_in(arg_keys[2], 2), own, number, FIB_DEV, N_SKY, 1, FIB_DEV * 5 // (4 * N_SKY), 2))(owner_keys, owner_turns).reshape((FIBRES, 1))
    offset = set_ends(jax.random.randint(arg_keys[3], (FIBRES,), 0, (NX // N_SKY) * NY), jax.random.fold_in(arg_keys[3], 1), 0, ((NX // N_SKY) * NY) - 1).astype(jnp.int32)
    return dict(spectra=spectra, kernel=kernel, owner=owner, offset=offset)


def dft_tables(length):
    steps = jnp.arange(length, dtype=jnp.int32)
    phase = steps[:, None] * steps[None, :] % length
    angles = phase.astype(jnp.float32) * (2.0 * math.pi / length)
    factor = 1.0 / math.sqrt(length)
    return ((jnp.cos(angles) * factor).astype(jnp.bfloat16), (jnp.sin(angles) * factor).astype(jnp.bfloat16))

def reference(spectra, kernel, owner, offset):
    tile_rows = NX // N_SKY
    corner_row = owner[:, 0] * tile_rows + offset // NY
    corner_col = offset % NY
    values = spectra.astype(jnp.float32)
    weights = kernel.astype(jnp.float32)
    flat = jnp.zeros((NX * NY, NW), jnp.float32)
    for step_a in range(KSIDE):
        for step_b in range(KSIDE):
            target = (corner_row + step_a) % NX * NY + (corner_col + step_b) % NY
            flat = flat.at[target.astype(jnp.int32)].add(weights[:, step_a * KSIDE + step_b][:, None] * values)
    cube = flat.reshape(NX, NY, NW).astype(jnp.bfloat16).astype(jnp.float32)
    cos_y, sin_y = dft_tables(NY)
    first_re = jnp.einsum('xyw,yk->xkw', cube, cos_y.astype(jnp.float32)).astype(jnp.bfloat16).astype(jnp.float32)
    first_im = (-jnp.einsum('xyw,yk->xkw', cube, sin_y.astype(jnp.float32))).astype(jnp.bfloat16).astype(jnp.float32)
    cos_w, sin_w = dft_tables(NW)
    cos_w = cos_w.astype(jnp.float32)
    sin_w = sin_w.astype(jnp.float32)
    second_re = (jnp.einsum('xkw,wv->xkv', first_re, cos_w) + jnp.einsum('xkw,wv->xkv', first_im, sin_w)).astype(jnp.bfloat16).astype(jnp.float32)
    second_im = (jnp.einsum('xkw,wv->xkv', first_im, cos_w) - jnp.einsum('xkw,wv->xkv', first_re, sin_w)).astype(jnp.bfloat16).astype(jnp.float32)
    cos_x, sin_x = dft_tables(NX)
    cos_x = cos_x.astype(jnp.float32)
    sin_x = sin_x.astype(jnp.float32)
    third_re = jnp.einsum('xkv,xu->ukv', second_re, cos_x) + jnp.einsum('xkv,xu->ukv', second_im, sin_x)
    third_im = jnp.einsum('xkv,xu->ukv', second_im, cos_x) - jnp.einsum('xkv,xu->ukv', second_re, sin_x)
    return jnp.stack([third_re, third_im])
```

```python
import math

import jax
import jax.numpy as jnp
import numpy as np
from jax import lax
from jax.sharding import PartitionSpec as P

NX = 256
NY = 256
NW = 1032
KSIDE = 4
BF = jnp.bfloat16
F32 = jnp.float32


def dft_tables(length):
    steps = np.arange(length)
    angles = (steps[:, None] * steps[None, :] % length).astype(np.float64) * (2.0 * math.pi / length)
    factor = 1.0 / math.sqrt(length)
    return np.cos(angles) * factor, np.sin(angles) * factor


def pack(spectra, kernel, owner, offset):
    sky_count, gz_count = lax.axis_size("sky"), lax.axis_size("gz")
    fibre_count, slab = spectra.shape
    cap = fibre_count * 5 // (4 * sky_count)
    slots = sky_count * cap
    own = owner[:, 0]
    order = jnp.arange(fibre_count, dtype=jnp.int32)
    earlier = (own[None, :] == own[:, None]) & (order[None, :] < order[:, None])
    position = own * cap + jnp.sum(earlier.astype(jnp.int32), axis=1)
    place = (jnp.arange(slots, dtype=jnp.int32)[:, None] == position[None, :]).astype(BF)
    tile_rows = NX // sky_count
    rows = (offset // NY).astype(BF)
    cols = (offset % NY).astype(BF)
    taps = KSIDE * KSIDE // gz_count
    own_taps = lax.dynamic_slice_in_dim(kernel, lax.axis_index("gz") * taps, taps, axis=1)
    wide = slab // 128 * 128
    main = jnp.dot(place, spectra[:, :wide], preferred_element_type=F32).astype(BF)
    rest = jnp.concatenate([spectra[:, wide:], own_taps, rows[:, None], cols[:, None]], axis=1)
    rest = lax.dot_general(rest, place, (((0,), (1,)), ((), ())), preferred_element_type=F32).astype(BF)
    per_row = -(-slots // wide)
    rest = jnp.pad(rest, ((0, -rest.shape[0] % 8), (0, per_row * wide - slots)))
    rest = rest.reshape(-1, wide)
    return jnp.concatenate([main, rest], axis=0), wide, per_row, cap


def shards(spectra, kernel, owner, offset):
    sky_count, gz_count = lax.axis_size("sky"), lax.axis_size("gz")
    slab = spectra.shape[1]
    tile_rows = NX // sky_count
    pad_rows = tile_rows + 8
    block, wide, per_row, cap = pack(spectra, kernel, owner, offset)
    slots = sky_count * cap
    got = lax.all_gather(block, ("sky", "gz"), axis=0, tiled=False)
    got = got.reshape(sky_count, gz_count, block.shape[0], wide)
    main = got[:, :, :slots].reshape(sky_count, gz_count, sky_count, cap, wide)
    main = main.transpose(2, 0, 3, 1, 4).reshape(sky_count, slots, gz_count * wide)
    rest = got[:, :, slots:].reshape(sky_count, gz_count, -1, per_row * wide)[:, :, :, :slots]
    rest = rest.reshape(sky_count, gz_count, -1, sky_count, cap)
    rest = rest.transpose(3, 0, 4, 1, 2).reshape(sky_count, slots, gz_count, -1)
    narrow = slab - wide
    taps = KSIDE * KSIDE // gz_count
    tail = rest[..., :narrow].reshape(sky_count, slots, gz_count * narrow)
    weights = rest[..., narrow : narrow + taps].reshape(sky_count, slots, KSIDE, KSIDE).astype(F32)
    row = rest[:, :, 0, narrow + taps].astype(jnp.int32)
    col = rest[:, :, 0, narrow + taps + 1].astype(jnp.int32)

    cos_w, sin_w = dft_tables(NW)
    table = np.concatenate([cos_w, -sin_w], axis=1).reshape(gz_count, slab, 2 * NW)
    table_main = jnp.asarray(table[:, :wide].reshape(gz_count * wide, 2 * NW), BF)
    table_tail = jnp.asarray(table[:, wide:].reshape(gz_count * narrow, 2 * NW), BF)
    lines = jnp.concatenate([main, tail], axis=-1)
    spec = jnp.einsum(
        "ojw,wv->ojv", lines, jnp.concatenate([table_main, table_tail]), preferred_element_type=F32
    ).astype(BF)

    per_block = NY // (sky_count * gz_count)
    first = (lax.axis_index("sky") * gz_count + lax.axis_index("gz")) * per_block
    freq = first + jnp.arange(per_block, dtype=jnp.int32)
    cells = col[:, None, :, None] + jnp.arange(KSIDE, dtype=jnp.int32)
    phase = (freq[None, :, None, None] * cells % NY).astype(F32) * (2.0 * math.pi / NY)
    factor = 1.0 / math.sqrt(NY)
    wave = jnp.stack([jnp.cos(phase), -jnp.sin(phase)], axis=1) * factor
    side = [
        sum(wave[..., b] * weights[:, None, None, :, a, b] for b in range(KSIDE))
        for a in range(KSIDE)
    ]
    lag = jnp.arange(pad_rows, dtype=jnp.int32)[None, :, None] - row[:, None, :]
    lag = lag[:, None, None]
    spread = sum(jnp.where(lag == a, side[a][:, :, :, None, :], 0.0) for a in range(KSIDE)).astype(BF)

    both = jnp.einsum("ozkrj,ojv->ozkrv", spread, spec, preferred_element_type=F32)
    plane_re = both[:, 0, ..., :NW] - both[:, 1, ..., NW:]
    plane_im = both[:, 0, ..., NW:] + both[:, 1, ..., :NW]
    planes = jnp.stack([plane_re, plane_im]).astype(BF)
    cos_x, sin_x = dft_tables(NX)
    held = (np.arange(sky_count)[:, None] * tile_rows + np.arange(pad_rows)[None, :]) % NX
    cos_x, sin_x = cos_x[held], sin_x[held]
    turn = np.stack([np.stack([cos_x, sin_x]), np.stack([-sin_x, cos_x])])
    return jnp.einsum("cokrv,zcoru->zukv", planes, jnp.asarray(turn, BF), preferred_element_type=F32)


def solution(mesh):
    in_specs = (P("sky", "gz"), P("sky", None), P("sky", None), P("sky"))
    out_specs = P(None, None, ("sky", "gz"), None)
    return jax.shard_map(shards, mesh=mesh, in_specs=in_specs, out_specs=out_specs, check_vma=False)
```

```python
import functools
import math

import jax
import jax.numpy as jnp
import numpy as np
from jax import lax
from jax.experimental import pallas as pl
from jax.experimental.pallas import tpu as pltpu
from jax.sharding import PartitionSpec as P

NX = 256
NY = 256
NW = 1032
KSIDE = 4
BF = jnp.bfloat16
F32 = jnp.float32
LANES = 128
INTERPRET = False


def dft_tables(length):
    steps = np.arange(length)
    angles = (steps[:, None] * steps[None, :] % length).astype(np.float64) * (2.0 * math.pi / length)
    factor = 1.0 / math.sqrt(length)
    return np.cos(angles) * factor, np.sin(angles) * factor


def pack(spectra, kernel, owner, offset):
    sky_count, gz_count = lax.axis_size("sky"), lax.axis_size("gz")
    fibre_count, slab = spectra.shape
    cap = -(-(fibre_count * 5 // (4 * sky_count)) // 8) * 8
    slots = sky_count * cap
    own = owner[:, 0]
    order = jnp.arange(fibre_count, dtype=jnp.int32)
    earlier = (own[None, :] == own[:, None]) & (order[None, :] < order[:, None])
    position = own * cap + jnp.sum(earlier.astype(jnp.int32), axis=1)
    place = (jnp.arange(slots, dtype=jnp.int32)[:, None] == position[None, :]).astype(BF)
    tile_rows = NX // sky_count
    rows = (offset // NY).astype(BF)
    cols = (offset % NY).astype(BF)
    taps = KSIDE * KSIDE // gz_count
    own_taps = lax.dynamic_slice_in_dim(kernel, lax.axis_index("gz") * taps, taps, axis=1)
    wide = slab // 128 * 128
    main = jnp.dot(place, spectra[:, :wide], preferred_element_type=F32).astype(BF)
    rest = jnp.concatenate([spectra[:, wide:], own_taps, rows[:, None], cols[:, None]], axis=1)
    rest = lax.dot_general(rest, place, (((0,), (1,)), ((), ())), preferred_element_type=F32).astype(BF)
    per_row = -(-slots // wide)
    rest = jnp.pad(rest, ((0, -rest.shape[0] % 8), (0, per_row * wide - slots)))
    rest = rest.reshape(-1, wide)
    return jnp.concatenate([main, rest], axis=0), wide, per_row, cap


def cube_kernel(dims, got_ref, tail_ref, wave_ref, spread_ref, turn_ref, out_ref, spec_ref, plane_ref):
    sky_count, gz_count, cap, wide, tile_rows, pad_rows, freqs = dims
    slots = sky_count * cap
    depth = gz_count * wide

    def transform(source, _):
        spec = jnp.dot(tail_ref[source], wave_ref[0, depth:], preferred_element_type=F32)
        for g in range(gz_count):
            lines = got_ref[source * gz_count + g, :slots, :]
            table = wave_ref[0, g * wide : (g + 1) * wide, :]
            spec = spec + jnp.dot(lines, table, preferred_element_type=F32)
        for o in range(sky_count):
            spec_ref[o, source] = spec[o * cap : (o + 1) * cap]
        return _

    lax.fori_loop(0, sky_count, transform, 0)
    plane_ref[:, :8] = jnp.zeros((freqs, 8, 2 * LANES), F32)

    def spread_out(o, _):
        spec = spec_ref[o].reshape(slots, 2 * LANES).astype(BF)
        both = jnp.dot(spread_ref[o], spec, preferred_element_type=F32)
        half = freqs * pad_rows
        first = pl.multiple_of(o * tile_rows, 8)
        for k in range(freqs):
            by_re = both[k * pad_rows : (k + 1) * pad_rows]
            by_im = both[half + k * pad_rows : half + (k + 1) * pad_rows]
            here = jnp.concatenate(
                [by_re[:, :LANES] - by_im[:, LANES:], by_re[:, LANES:] + by_im[:, :LANES]], axis=1
            )
            plane_ref[k, pl.ds(first, 8)] += here[:8]
            plane_ref[k, pl.ds(first + 8, tile_rows)] = here[8:]
        return _

    lax.fori_loop(0, sky_count, spread_out, 0)
    for k in range(freqs):
        plane_ref[k, :8] += plane_ref[k, NX : NX + 8]
        turned = jnp.dot(turn_ref[...], plane_ref[k, :NX].astype(BF), preferred_element_type=F32)
        out_ref[pl.ds(k, NX, stride=freqs), :] = turned[:NX, :LANES] + turned[NX:, LANES:]
        out_ref[pl.ds(NX * freqs + k, NX, stride=freqs), :] = turned[:NX, LANES:] - turned[NX:, :LANES]


def shards(spectra, kernel, owner, offset):
    sky_count, gz_count = lax.axis_size("sky"), lax.axis_size("gz")
    slab = spectra.shape[1]
    tile_rows = NX // sky_count
    pad_rows = tile_rows + 8
    block, wide, per_row, cap = pack(spectra, kernel, owner, offset)
    slots = sky_count * cap
    got = lax.all_gather(block, ("sky", "gz"), axis=0, tiled=False)
    rest = got[:, slots:].reshape(sky_count, gz_count, -1, per_row * wide)[:, :, :, :slots]
    narrow = slab - wide
    taps = KSIDE * KSIDE // gz_count
    tail = rest[:, :, :narrow].reshape(sky_count, gz_count * narrow, slots).transpose(0, 2, 1)

    def by_owner(item):
        item = item.reshape(-1, sky_count, cap).reshape(sky_count, -1, sky_count, cap)
        return item.transpose(2, 1, 0, 3).reshape(sky_count, -1, slots)

    weights = by_owner(rest[:, :, narrow : narrow + taps]).astype(F32)
    row = by_owner(rest[:, 0, narrow + taps])[:, 0].astype(jnp.int32)
    col = by_owner(rest[:, 0, narrow + taps + 1])[:, 0].astype(jnp.int32)

    per_block = NY // (sky_count * gz_count)
    first = (lax.axis_index("sky") * gz_count + lax.axis_index("gz")) * per_block
    freq = first + jnp.arange(per_block, dtype=jnp.int32)
    factor = 1.0 / math.sqrt(NY)
    side = [0.0] * KSIDE
    for b in range(KSIDE):
        phase = (freq[None, :, None] * (col + b)[:, None, :] % NY).astype(F32) * (2.0 * math.pi / NY)
        wave = jnp.stack([jnp.cos(phase), -jnp.sin(phase)], axis=1) * factor
        for a in range(KSIDE):
            side[a] = side[a] + wave * weights[:, None, None, a * KSIDE + b]
    lag = jnp.arange(pad_rows, dtype=jnp.int32)[None, :, None] - row[:, None, :]
    lag = lag[:, None, None]
    spread = jnp.zeros((), F32)
    for a in range(KSIDE):
        spread = jnp.where(lag == a, side[a][:, :, :, None, :], spread)
    spread = spread.astype(BF).reshape(sky_count, 2 * per_block * pad_rows, slots)

    chunks = -(-NW // LANES)
    cos_w, sin_w = dft_tables(NW)
    wave_table = np.zeros((NW, 2, chunks * LANES), np.float32)
    wave_table[:, 0, :NW], wave_table[:, 1, :NW] = cos_w, -sin_w
    wave_table = wave_table.reshape(gz_count, slab, 2, chunks, LANES)
    wave_table = np.concatenate(
        [
            wave_table[:, :wide].reshape(gz_count * wide, 2, chunks, LANES),
            wave_table[:, wide:].reshape(gz_count * narrow, 2, chunks, LANES),
        ]
    )
    wave_table = wave_table.transpose(2, 0, 1, 3).reshape(chunks, NW, 2 * LANES)
    turn = np.concatenate(dft_tables(NX))

    dims = (sky_count, gz_count, cap, wide, tile_rows, pad_rows, per_block)
    macs = chunks * 2 * LANES * sky_count * slots * (NW + 2 * per_block * pad_rows)
    macs += chunks * 2 * LANES * 2 * NX * NX * per_block
    result = pl.pallas_call(
        functools.partial(cube_kernel, dims),
        grid=(chunks,),
        in_specs=[
            pl.BlockSpec(got.shape, lambda i: (0, 0, 0)),
            pl.BlockSpec(tail.shape, lambda i: (0, 0, 0)),
            pl.BlockSpec((1, NW, 2 * LANES), lambda i: (i, 0, 0)),
            pl.BlockSpec(spread.shape, lambda i: (0, 0, 0)),
            pl.BlockSpec(turn.shape, lambda i: (0, 0)),
        ],
        out_specs=pl.BlockSpec((2 * NX * per_block, LANES), lambda i: (0, i)),
        out_shape=jax.ShapeDtypeStruct((2 * NX * per_block, NW), F32),
        scratch_shapes=[
            pltpu.VMEM((sky_count, sky_count, cap, 2 * LANES), F32),
            pltpu.VMEM((per_block, NX + 8, 2 * LANES), F32),
        ],
        compiler_params=pltpu.CompilerParams(vmem_limit_bytes=56 * 1024 * 1024),
        cost_estimate=pl.CostEstimate(flops=2 * macs, bytes_accessed=32 * 1024 * 1024, transcendentals=0),
        interpret=INTERPRET,
    )(got, tail, jnp.asarray(wave_table, BF), spread, jnp.asarray(turn, BF))
    return result.reshape(2, NX, per_block, NW)


def solution(mesh):
    in_specs = (P("sky", "gz"), P("sky", None), P("sky", None), P("sky"))
    out_specs = P(None, None, ("sky", "gz"), None)
    return jax.shard_map(shards, mesh=mesh, in_specs=in_specs, out_specs=out_specs, check_vma=False)
```

```python
import functools
import math

import jax
import jax.numpy as jnp
import numpy as np
from jax import lax
from jax.experimental import pallas as pl
from jax.experimental.pallas import tpu as pltpu
from jax.sharding import PartitionSpec as P

NX = 256
NY = 256
NW = 1032
KSIDE = 4
BF = jnp.bfloat16
F32 = jnp.float32
WIDTH = 384
INTERPRET = False


def dft_tables(length):
    steps = np.arange(length)
    angles = (steps[:, None] * steps[None, :] % length).astype(np.float64) * (2.0 * math.pi / length)
    factor = 1.0 / math.sqrt(length)
    return np.cos(angles) * factor, np.sin(angles) * factor


def pack(spectra, kernel, owner, offset):
    sky_count, gz_count = lax.axis_size("sky"), lax.axis_size("gz")
    fibre_count, slab = spectra.shape
    cap = -(-(fibre_count * 5 // (4 * sky_count)) // 8) * 8
    slots = sky_count * cap
    own = owner[:, 0]
    order = jnp.arange(fibre_count, dtype=jnp.int32)
    earlier = (own[None, :] == own[:, None]) & (order[None, :] < order[:, None])
    position = own * cap + jnp.sum(earlier.astype(jnp.int32), axis=1)
    place = (jnp.arange(slots, dtype=jnp.int32)[:, None] == position[None, :]).astype(BF)
    tile_rows = NX // sky_count
    rows = (offset // NY).astype(BF)
    cols = (offset % NY).astype(BF)
    taps = KSIDE * KSIDE // gz_count
    own_taps = lax.dynamic_slice_in_dim(kernel, lax.axis_index("gz") * taps, taps, axis=1)
    wide = slab // 128 * 128
    main = jnp.dot(place, spectra[:, :wide], preferred_element_type=F32).astype(BF)
    rest = jnp.concatenate([spectra[:, wide:], own_taps, rows[:, None], cols[:, None]], axis=1)
    rest = lax.dot_general(rest, place, (((0,), (1,)), ((), ())), preferred_element_type=F32).astype(BF)
    per_row = -(-slots // wide)
    rest = jnp.pad(rest, ((0, -rest.shape[0] % 8), (0, per_row * wide - slots)))
    rest = rest.reshape(-1, wide)
    return jnp.concatenate([main, rest], axis=0), wide, per_row, cap


def cube_kernel(dims, got_ref, tail_ref, wave_ref, spread_ref, turn_ref, out_ref, spec_ref, plane_ref):
    sky_count, gz_count, cap, wide, tile_rows, pad_rows, freqs = dims
    slots = sky_count * cap
    depth = gz_count * wide
    pair = 2

    def transform(step, _):
        lines = jnp.concatenate(
            [
                jnp.concatenate(
                    [got_ref[(step * pair + i) * gz_count + g, :slots, :] for i in range(pair)], axis=0
                )
                for g in range(gz_count)
            ],
            axis=1,
        )
        tail = jnp.concatenate([tail_ref[step * pair + i] for i in range(pair)], axis=0)
        spec = jnp.dot(lines, wave_ref[0, :depth], preferred_element_type=F32)
        spec = spec + jnp.dot(tail, wave_ref[0, depth:], preferred_element_type=F32)
        for i in range(pair):
            for o in range(sky_count):
                start = i * slots + o * cap
                spec_ref[o, step * pair + i] = spec[start : start + cap]
        return _

    lax.fori_loop(0, sky_count // pair, transform, 0)
    plane_ref[:, :8] = jnp.zeros((freqs, 8, 2 * WIDTH), F32)

    def spread_out(o, _):
        spec = spec_ref[o].reshape(slots, 2 * WIDTH).astype(BF)
        both = jnp.dot(spread_ref[o], spec, preferred_element_type=F32)
        half = freqs * pad_rows
        first = pl.multiple_of(o * tile_rows, 8)
        for k in range(freqs):
            by_re = both[k * pad_rows : (k + 1) * pad_rows]
            by_im = both[half + k * pad_rows : half + (k + 1) * pad_rows]
            here = jnp.concatenate(
                [by_re[:, :WIDTH] - by_im[:, WIDTH:], by_re[:, WIDTH:] + by_im[:, :WIDTH]], axis=1
            )
            plane_ref[k, pl.ds(first, 8)] += here[:8]
            plane_ref[k, pl.ds(first + 8, tile_rows)] = here[8:]
        return _

    lax.fori_loop(0, sky_count, spread_out, 0)

    def turn_rows(k, _):
        plane_ref[k, :8] += plane_ref[k, NX : NX + 8]
        plane = plane_ref[k, :NX].astype(BF)
        turned = lax.dot_general(
            plane, turn_ref[...], (((0,), (0,)), ((), ())), preferred_element_type=F32
        )
        out_ref[0, k] = turned[:WIDTH, :NX] + turned[WIDTH:, NX:]
        out_ref[1, k] = turned[WIDTH:, :NX] - turned[:WIDTH, NX:]
        return _

    lax.fori_loop(0, freqs, turn_rows, 0)


def shards(spectra, kernel, owner, offset):
    sky_count, gz_count = lax.axis_size("sky"), lax.axis_size("gz")
    slab = spectra.shape[1]
    tile_rows = NX // sky_count
    pad_rows = tile_rows + 8
    block, wide, per_row, cap = pack(spectra, kernel, owner, offset)
    slots = sky_count * cap
    got = lax.all_gather(block, ("sky", "gz"), axis=0, tiled=False)
    rest = got[:, slots:].reshape(sky_count, gz_count, -1, per_row * wide)[:, :, :, :slots]
    narrow = slab - wide
    taps = KSIDE * KSIDE // gz_count
    tail = rest[:, :, :narrow].reshape(sky_count, gz_count * narrow, slots).transpose(0, 2, 1)

    def by_owner(item):
        item = item.reshape(-1, sky_count, cap).reshape(sky_count, -1, sky_count, cap)
        return item.transpose(2, 1, 0, 3).reshape(sky_count, -1, slots)

    weights = by_owner(rest[:, :, narrow : narrow + taps]).astype(F32)
    row = by_owner(rest[:, 0, narrow + taps])[:, 0].astype(jnp.int32)
    col = by_owner(rest[:, 0, narrow + taps + 1])[:, 0].astype(jnp.int32)

    per_block = NY // (sky_count * gz_count)
    first = (lax.axis_index("sky") * gz_count + lax.axis_index("gz")) * per_block
    freq = first + jnp.arange(per_block, dtype=jnp.int32)
    factor = 1.0 / math.sqrt(NY)
    side = [0.0] * KSIDE
    for b in range(KSIDE):
        phase = (freq[None, :, None] * (col + b)[:, None, :] % NY).astype(F32) * (2.0 * math.pi / NY)
        wave = jnp.stack([jnp.cos(phase), -jnp.sin(phase)], axis=1) * factor
        for a in range(KSIDE):
            side[a] = side[a] + wave * weights[:, None, None, a * KSIDE + b]
    lag = jnp.arange(pad_rows, dtype=jnp.int32)[None, :, None] - row[:, None, :]
    lag = lag[:, None, None]
    spread = jnp.zeros((), F32)
    for a in range(KSIDE):
        spread = jnp.where(lag == a, side[a][:, :, :, None, :], spread)
    spread = spread.astype(BF).reshape(sky_count, 2 * per_block * pad_rows, slots)

    chunks = -(-NW // WIDTH)
    cos_w, sin_w = dft_tables(NW)
    wave_table = np.zeros((NW, 2, chunks * WIDTH), np.float32)
    wave_table[:, 0, :NW], wave_table[:, 1, :NW] = cos_w, -sin_w
    wave_table = wave_table.reshape(gz_count, slab, 2, chunks, WIDTH)
    wave_table = np.concatenate(
        [
            wave_table[:, :wide].reshape(gz_count * wide, 2, chunks, WIDTH),
            wave_table[:, wide:].reshape(gz_count * narrow, 2, chunks, WIDTH),
        ]
    )
    wave_table = wave_table.transpose(2, 0, 1, 3).reshape(chunks, NW, 2 * WIDTH)
    turn = np.concatenate(dft_tables(NX), axis=1)

    dims = (sky_count, gz_count, cap, wide, tile_rows, pad_rows, per_block)
    macs = chunks * 2 * WIDTH * sky_count * slots * (NW + 2 * per_block * pad_rows)
    macs += chunks * 2 * WIDTH * 2 * NX * NX * per_block
    result = pl.pallas_call(
        functools.partial(cube_kernel, dims),
        grid=(chunks,),
        in_specs=[
            pl.BlockSpec(got.shape, lambda i: (0, 0, 0), pipeline_mode=pl.Buffered(1)),
            pl.BlockSpec(tail.shape, lambda i: (0, 0, 0), pipeline_mode=pl.Buffered(1)),
            pl.BlockSpec((1, NW, 2 * WIDTH), lambda i: (i, 0, 0)),
            pl.BlockSpec(spread.shape, lambda i: (0, 0, 0), pipeline_mode=pl.Buffered(1)),
            pl.BlockSpec(turn.shape, lambda i: (0, 0)),
        ],
        out_specs=pl.BlockSpec((2, per_block, WIDTH, NX), lambda i: (0, 0, i, 0)),
        out_shape=jax.ShapeDtypeStruct((2, per_block, NW, NX), F32),
        scratch_shapes=[
            pltpu.VMEM((sky_count, sky_count, cap, 2 * WIDTH), F32),
            pltpu.VMEM((per_block, NX + 8, 2 * WIDTH), F32),
        ],
        compiler_params=pltpu.CompilerParams(vmem_limit_bytes=56 * 1024 * 1024),
        cost_estimate=pl.CostEstimate(flops=2 * macs, bytes_accessed=32 * 1024 * 1024, transcendentals=0),
        interpret=INTERPRET,
    )(got, tail, jnp.asarray(wave_table, BF), spread, jnp.asarray(turn, BF))
    return result.transpose(0, 3, 1, 2)


def solution(mesh):
    in_specs = (P("sky", "gz"), P("sky", None), P("sky", None), P("sky"))
    out_specs = P(None, None, ("sky", "gz"), None)
    return jax.shard_map(shards, mesh=mesh, in_specs=in_specs, out_specs=out_specs, check_vma=False)
```

```python
import functools
import math

import jax
import jax.numpy as jnp
import numpy as np
from jax import lax
from jax.experimental import pallas as pl
from jax.experimental.pallas import tpu as pltpu
from jax.sharding import PartitionSpec as P

NX = 256
NY = 256
NW = 1032
KSIDE = 4
BF = jnp.bfloat16
F32 = jnp.float32
WIDTH = 384
INTERPRET = False


def dft_tables(length):
    steps = np.arange(length)
    angles = (steps[:, None] * steps[None, :] % length).astype(np.float64) * (2.0 * math.pi / length)
    factor = 1.0 / math.sqrt(length)
    return np.cos(angles) * factor, np.sin(angles) * factor


def pack(spectra, kernel, owner, offset):
    sky_count, gz_count = lax.axis_size("sky"), lax.axis_size("gz")
    fibre_count, slab = spectra.shape
    cap = -(-(fibre_count * 5 // (4 * sky_count)) // 8) * 8
    slots = sky_count * cap
    own = owner[:, 0]
    order = jnp.arange(fibre_count, dtype=jnp.int32)
    earlier = (own[None, :] == own[:, None]) & (order[None, :] < order[:, None])
    position = own * cap + jnp.sum(earlier.astype(jnp.int32), axis=1)
    place = (jnp.arange(slots, dtype=jnp.int32)[:, None] == position[None, :]).astype(BF)
    tile_rows = NX // sky_count
    rows = (offset // NY).astype(BF)
    cols = (offset % NY).astype(BF)
    taps = KSIDE * KSIDE // gz_count
    own_taps = lax.dynamic_slice_in_dim(kernel, lax.axis_index("gz") * taps, taps, axis=1)
    wide = slab // 128 * 128
    main = jnp.dot(place, spectra[:, :wide], preferred_element_type=F32).astype(BF)
    rest = jnp.concatenate([spectra[:, wide:], own_taps, rows[:, None], cols[:, None]], axis=1)
    rest = lax.dot_general(rest, place, (((0,), (1,)), ((), ())), preferred_element_type=F32).astype(BF)
    per_row = -(-slots // wide)
    rest = jnp.pad(rest, ((0, -rest.shape[0] % 8), (0, per_row * wide - slots)))
    rest = rest.reshape(-1, wide)
    rest = jnp.pad(rest, ((0, -(slots + rest.shape[0]) % 16), (0, 0)))
    return jnp.concatenate([main, rest], axis=0), wide, per_row, cap


def gather_kernel(sky_count, gz_count, block_ref, all_ref, send_sem, recv_sem, own_sem):
    me, z = lax.axis_index("sky"), lax.axis_index("gz")
    rows = block_ref.shape[0]
    cut = (rows // 2 + 15) // 16 * 16
    bits = [1 << i for i in range(1, sky_count.bit_length() - 1)]

    def flipped(index, p):
        return index + p * (1 - 2 * ((me // p) % 2))

    barrier = pltpu.get_barrier_semaphore()
    near = [(me, lax.rem(z + i, gz_count)) for i in range(1, gz_count)]
    far = [(flipped(me, p), z) for p in [1] + bits]
    for device in near + far:
        pl.semaphore_signal(barrier, inc=1, device_id=device, device_id_type=pl.DeviceIdType.MESH)
    pl.semaphore_wait(barrier, len(near) + len(far))

    started = []

    def send(source, target, device):
        number = len(started)
        copy = pltpu.make_async_remote_copy(
            src_ref=source,
            dst_ref=target,
            send_sem=send_sem.at[number],
            recv_sem=recv_sem.at[number],
            device_id=device,
            device_id_type=pl.DeviceIdType.MESH,
        )
        copy.start()
        started.append(copy)
        return copy

    def piece(group, start, size):
        return all_ref.at[pl.ds(group * gz_count, gz_count), pl.ds(start, size)]

    mine = all_ref.at[me * gz_count + z]
    own = pltpu.make_async_copy(block_ref, mine, own_sem)
    own.start()
    first = [send(block_ref, mine, device) for device in near]
    own.wait()
    for copy in first:
        copy.wait_recv()
    across = (flipped(me, 1), z)
    whole = piece(me, 0, rows)
    last = [send(whole, whole, across)]
    halves = [(0, cut, bits), (cut, rows - cut, bits[::-1])]
    held = [[me], [me]]
    for step in range(len(bits)):
        coming = []
        for h, (start, size, order) in enumerate(halves):
            device = (flipped(me, order[step]), z)
            coming.append(
                [send(piece(g, start, size), piece(g, start, size), device) for g in held[h]]
            )
        for h, (start, size, order) in enumerate(halves):
            new = [flipped(g, order[step]) for g in held[h]]
            for copy, g in zip(coming[h], new):
                copy.wait_recv()
                last.append(send(piece(g, start, size), piece(g, start, size), across))
            held[h] = held[h] + new
    for copy in last:
        copy.wait_recv()
    for copy in started:
        copy.wait_send()


def gather(block, sky_count, gz_count):
    copies = gz_count - 1 + 1 + 4 * (sky_count // 2 - 1)
    return pl.pallas_call(
        functools.partial(gather_kernel, sky_count, gz_count),
        out_shape=jax.ShapeDtypeStruct((sky_count * gz_count,) + block.shape, block.dtype),
        in_specs=[pl.BlockSpec(memory_space=pl.ANY)],
        out_specs=pl.BlockSpec(memory_space=pl.ANY),
        scratch_shapes=[
            pltpu.SemaphoreType.DMA((copies,)),
            pltpu.SemaphoreType.DMA((copies,)),
            pltpu.SemaphoreType.DMA,
        ],
        compiler_params=pltpu.CompilerParams(collective_id=0, has_side_effects=True),
    )(block)


def cube_kernel(dims, got_ref, tail_ref, wave_ref, spread_ref, turn_ref, out_ref, spec_ref, plane_ref):
    sky_count, gz_count, cap, wide, tile_rows, pad_rows, freqs = dims
    slots = sky_count * cap
    depth = gz_count * wide
    pair = 2

    def transform(step, _):
        lines = jnp.concatenate(
            [
                jnp.concatenate(
                    [got_ref[(step * pair + i) * gz_count + g, :slots, :] for i in range(pair)], axis=0
                )
                for g in range(gz_count)
            ],
            axis=1,
        )
        tail = jnp.concatenate([tail_ref[step * pair + i] for i in range(pair)], axis=0)
        spec = jnp.dot(lines, wave_ref[0, :depth], preferred_element_type=F32)
        spec = spec + jnp.dot(tail, wave_ref[0, depth:], preferred_element_type=F32)
        for i in range(pair):
            for o in range(sky_count):
                start = i * slots + o * cap
                spec_ref[o, step * pair + i] = spec[start : start + cap]
        return _

    lax.fori_loop(0, sky_count // pair, transform, 0)
    plane_ref[:, :8] = jnp.zeros((freqs, 8, 2 * WIDTH), F32)

    def spread_out(o, _):
        spec = spec_ref[o].reshape(slots, 2 * WIDTH).astype(BF)
        both = jnp.dot(spread_ref[o], spec, preferred_element_type=F32)
        half = freqs * pad_rows
        first = pl.multiple_of(o * tile_rows, 8)
        for k in range(freqs):
            by_re = both[k * pad_rows : (k + 1) * pad_rows]
            by_im = both[half + k * pad_rows : half + (k + 1) * pad_rows]
            here = jnp.concatenate(
                [by_re[:, :WIDTH] - by_im[:, WIDTH:], by_re[:, WIDTH:] + by_im[:, :WIDTH]], axis=1
            )
            plane_ref[k, pl.ds(first, 8)] += here[:8]
            plane_ref[k, pl.ds(first + 8, tile_rows)] = here[8:]
        return _

    lax.fori_loop(0, sky_count, spread_out, 0)

    def turn_rows(k, _):
        plane_ref[k, :8] += plane_ref[k, NX : NX + 8]
        plane = plane_ref[k, :NX].astype(BF)
        turned = lax.dot_general(
            plane, turn_ref[...], (((0,), (0,)), ((), ())), preferred_element_type=F32
        )
        out_ref[0, k] = turned[:WIDTH, :NX] + turned[WIDTH:, NX:]
        out_ref[1, k] = turned[WIDTH:, :NX] - turned[:WIDTH, NX:]
        return _

    lax.fori_loop(0, freqs, turn_rows, 0)


def shards(spectra, kernel, owner, offset):
    sky_count, gz_count = lax.axis_size("sky"), lax.axis_size("gz")
    slab = spectra.shape[1]
    tile_rows = NX // sky_count
    pad_rows = tile_rows + 8
    block, wide, per_row, cap = pack(spectra, kernel, owner, offset)
    slots = sky_count * cap
    got = gather(block, sky_count, gz_count)
    rest = got[:, slots : slots + (block.shape[0] - slots) // per_row * per_row].reshape(sky_count, gz_count, -1, per_row * wide)[:, :, :, :slots]
    narrow = slab - wide
    taps = KSIDE * KSIDE // gz_count
    tail = rest[:, :, :narrow].reshape(sky_count, gz_count * narrow, slots).transpose(0, 2, 1)

    def by_owner(item):
        item = item.reshape(-1, sky_count, cap).reshape(sky_count, -1, sky_count, cap)
        return item.transpose(2, 1, 0, 3).reshape(sky_count, -1, slots)

    weights = by_owner(rest[:, :, narrow : narrow + taps]).astype(F32)
    row = by_owner(rest[:, 0, narrow + taps])[:, 0].astype(jnp.int32)
    col = by_owner(rest[:, 0, narrow + taps + 1])[:, 0].astype(jnp.int32)

    per_block = NY // (sky_count * gz_count)
    first = (lax.axis_index("sky") * gz_count + lax.axis_index("gz")) * per_block
    freq = first + jnp.arange(per_block, dtype=jnp.int32)
    factor = 1.0 / math.sqrt(NY)
    side = [0.0] * KSIDE
    for b in range(KSIDE):
        phase = (freq[None, :, None] * (col + b)[:, None, :] % NY).astype(F32) * (2.0 * math.pi / NY)
        wave = jnp.stack([jnp.cos(phase), -jnp.sin(phase)], axis=1) * factor
        for a in range(KSIDE):
            side[a] = side[a] + wave * weights[:, None, None, a * KSIDE + b]
    lag = jnp.arange(pad_rows, dtype=jnp.int32)[None, :, None] - row[:, None, :]
    lag = lag[:, None, None]
    spread = jnp.zeros((), F32)
    for a in range(KSIDE):
        spread = jnp.where(lag == a, side[a][:, :, :, None, :], spread)
    spread = spread.astype(BF).reshape(sky_count, 2 * per_block * pad_rows, slots)

    chunks = -(-NW // WIDTH)
    cos_w, sin_w = dft_tables(NW)
    wave_table = np.zeros((NW, 2, chunks * WIDTH), np.float32)
    wave_table[:, 0, :NW], wave_table[:, 1, :NW] = cos_w, -sin_w
    wave_table = wave_table.reshape(gz_count, slab, 2, chunks, WIDTH)
    wave_table = np.concatenate(
        [
            wave_table[:, :wide].reshape(gz_count * wide, 2, chunks, WIDTH),
            wave_table[:, wide:].reshape(gz_count * narrow, 2, chunks, WIDTH),
        ]
    )
    wave_table = wave_table.transpose(2, 0, 1, 3).reshape(chunks, NW, 2 * WIDTH)
    turn = np.concatenate(dft_tables(NX), axis=1)

    dims = (sky_count, gz_count, cap, wide, tile_rows, pad_rows, per_block)
    macs = chunks * 2 * WIDTH * sky_count * slots * (NW + 2 * per_block * pad_rows)
    macs += chunks * 2 * WIDTH * 2 * NX * NX * per_block
    result = pl.pallas_call(
        functools.partial(cube_kernel, dims),
        grid=(chunks,),
        in_specs=[
            pl.BlockSpec(got.shape, lambda i: (0, 0, 0), pipeline_mode=pl.Buffered(1)),
            pl.BlockSpec(tail.shape, lambda i: (0, 0, 0), pipeline_mode=pl.Buffered(1)),
            pl.BlockSpec((1, NW, 2 * WIDTH), lambda i: (i, 0, 0)),
            pl.BlockSpec(spread.shape, lambda i: (0, 0, 0), pipeline_mode=pl.Buffered(1)),
            pl.BlockSpec(turn.shape, lambda i: (0, 0)),
        ],
        out_specs=pl.BlockSpec((2, per_block, WIDTH, NX), lambda i: (0, 0, i, 0)),
        out_shape=jax.ShapeDtypeStruct((2, per_block, NW, NX), F32),
        scratch_shapes=[
            pltpu.VMEM((sky_count, sky_count, cap, 2 * WIDTH), F32),
            pltpu.VMEM((per_block, NX + 8, 2 * WIDTH), F32),
        ],
        compiler_params=pltpu.CompilerParams(vmem_limit_bytes=56 * 1024 * 1024),
        cost_estimate=pl.CostEstimate(flops=2 * macs, bytes_accessed=32 * 1024 * 1024, transcendentals=0),
        interpret=INTERPRET,
    )(got, tail, jnp.asarray(wave_table, BF), spread, jnp.asarray(turn, BF))
    return result.transpose(0, 3, 1, 2)


def solution(mesh):
    in_specs = (P("sky", "gz"), P("sky", None), P("sky", None), P("sky"))
    out_specs = P(None, None, ("sky", "gz"), None)
    return jax.shard_map(shards, mesh=mesh, in_specs=in_specs, out_specs=out_specs, check_vma=False)
```

```python
import functools
import math

import jax
import jax.numpy as jnp
import numpy as np
from jax import lax
from jax.experimental import pallas as pl
from jax.experimental.pallas import tpu as pltpu
from jax.sharding import PartitionSpec as P

NX = 256
NY = 256
NW = 1032
KSIDE = 4
BF = jnp.bfloat16
F32 = jnp.float32
WIDTH = 384
INTERPRET = False


def dft_tables(length):
    steps = np.arange(length)
    angles = (steps[:, None] * steps[None, :] % length).astype(np.float64) * (2.0 * math.pi / length)
    factor = 1.0 / math.sqrt(length)
    return np.cos(angles) * factor, np.sin(angles) * factor


def pack(spectra, kernel, owner, offset):
    sky_count, gz_count = lax.axis_size("sky"), lax.axis_size("gz")
    fibre_count, slab = spectra.shape
    cap = -(-(fibre_count * 5 // (4 * sky_count)) // 8) * 8
    slots = sky_count * cap
    own = owner[:, 0]
    order = jnp.arange(fibre_count, dtype=jnp.int32)
    earlier = (own[None, :] == own[:, None]) & (order[None, :] < order[:, None])
    position = own * cap + jnp.sum(earlier.astype(jnp.int32), axis=1)
    place = (jnp.arange(slots, dtype=jnp.int32)[:, None] == position[None, :]).astype(BF)
    tile_rows = NX // sky_count
    rows = (offset // NY).astype(BF)
    cols = (offset % NY).astype(BF)
    taps = KSIDE * KSIDE // gz_count
    own_taps = lax.dynamic_slice_in_dim(kernel, lax.axis_index("gz") * taps, taps, axis=1)
    wide = slab // 128 * 128
    main = jnp.dot(place, spectra[:, :wide], preferred_element_type=F32).astype(BF)
    rest = jnp.concatenate([spectra[:, wide:], own_taps, rows[:, None], cols[:, None]], axis=1)
    rest = lax.dot_general(rest, place, (((0,), (1,)), ((), ())), preferred_element_type=F32).astype(BF)
    per_row = -(-slots // wide)
    rest = jnp.pad(rest, ((0, -rest.shape[0] % 8), (0, per_row * wide - slots)))
    rest = rest.reshape(-1, wide)
    rest = jnp.pad(rest, ((0, -(slots + rest.shape[0]) % 16), (0, 0)))
    return jnp.concatenate([main, rest], axis=0), wide, per_row, cap


def gather_kernel(sky_count, gz_count, block_ref, all_ref, send_sem, recv_sem, own_sem):
    me, z = lax.axis_index("sky"), lax.axis_index("gz")
    rows = block_ref.shape[0]
    cut = (rows // 2 + 15) // 16 * 16
    bits = [1 << i for i in range(1, sky_count.bit_length() - 1)]

    def flipped(index, p):
        return index + p * (1 - 2 * ((me // p) % 2))

    barrier = pltpu.get_barrier_semaphore()
    near = [(me, lax.rem(z + i, gz_count)) for i in range(1, gz_count)]
    far = [(flipped(me, p), z) for p in [1] + bits]
    for device in near + far:
        pl.semaphore_signal(barrier, inc=1, device_id=device, device_id_type=pl.DeviceIdType.MESH)
    pl.semaphore_wait(barrier, len(near) + len(far))

    started = []

    def send(source, target, device):
        number = len(started)
        copy = pltpu.make_async_remote_copy(
            src_ref=source,
            dst_ref=target,
            send_sem=send_sem.at[number],
            recv_sem=recv_sem.at[number],
            device_id=device,
            device_id_type=pl.DeviceIdType.MESH,
        )
        copy.start()
        started.append(copy)
        return copy

    def piece(group, start, size):
        return all_ref.at[group[0] * gz_count + group[1], pl.ds(start, size)]

    mine = all_ref.at[me * gz_count + z]
    own = pltpu.make_async_copy(block_ref, mine, own_sem)
    own.start()
    first = [send(block_ref, mine, device) for device in near]
    across = (flipped(me, 1), z)
    halves = [(0, cut, bits), (cut, rows - cut, bits[::-1])]
    lines = [lax.rem(z + gz_count - i, gz_count) for i in range(gz_count)]
    last = []
    held = [[[(me, line)], [(me, line)]] for line in lines]
    coming = [None] * gz_count

    def go_on(i, step):
        coming[i] = []
        for h, (start, size, order) in enumerate(halves):
            device = (flipped(me, order[step]), z)
            coming[i].append(
                [send(piece(g, start, size), piece(g, start, size), device) for g in held[i][h]]
            )

    for i, line in enumerate(lines):
        if i == 0:
            own.wait()
        else:
            first[i - 1].wait_recv()
        go_on(i, 0)
        whole = piece((me, line), 0, rows)
        last.append(send(whole, whole, across))
    for step in range(len(bits)):
        for i in range(gz_count):
            arrived = []
            for h, (start, size, order) in enumerate(halves):
                new = [(flipped(g, order[step]), line) for g, line in held[i][h]]
                for copy in coming[i][h]:
                    copy.wait_recv()
                held[i][h] = held[i][h] + new
                arrived += [(g, start, size) for g in new]
            if step + 1 < len(bits):
                go_on(i, step + 1)
            for part in arrived:
                last.append(send(piece(*part), piece(*part), across))
    for copy in last:
        copy.wait_recv()
    for copy in started:
        copy.wait_send()


def gather(block, sky_count, gz_count):
    copies = gz_count - 1 + gz_count * (1 + 4 * (sky_count // 2 - 1))
    return pl.pallas_call(
        functools.partial(gather_kernel, sky_count, gz_count),
        out_shape=jax.ShapeDtypeStruct((sky_count * gz_count,) + block.shape, block.dtype),
        in_specs=[pl.BlockSpec(memory_space=pl.ANY)],
        out_specs=pl.BlockSpec(memory_space=pl.ANY),
        scratch_shapes=[
            pltpu.SemaphoreType.DMA((copies,)),
            pltpu.SemaphoreType.DMA((copies,)),
            pltpu.SemaphoreType.DMA,
        ],
        compiler_params=pltpu.CompilerParams(collective_id=0, has_side_effects=True),
    )(block)


def cube_kernel(dims, got_ref, tail_ref, wave_ref, spread_ref, turn_ref, out_ref, spec_ref, plane_ref):
    sky_count, gz_count, cap, wide, tile_rows, pad_rows, freqs = dims
    slots = sky_count * cap
    depth = gz_count * wide
    pair = 2

    def transform(step, _):
        lines = jnp.concatenate(
            [
                jnp.concatenate(
                    [got_ref[(step * pair + i) * gz_count + g, :slots, :] for i in range(pair)], axis=0
                )
                for g in range(gz_count)
            ],
            axis=1,
        )
        tail = jnp.concatenate([tail_ref[step * pair + i] for i in range(pair)], axis=0)
        spec = jnp.dot(lines, wave_ref[0, :depth], preferred_element_type=F32)
        spec = spec + jnp.dot(tail, wave_ref[0, depth:], preferred_element_type=F32)
        for i in range(pair):
            for o in range(sky_count):
                start = i * slots + o * cap
                spec_ref[o, step * pair + i] = spec[start : start + cap]
        return _

    lax.fori_loop(0, sky_count // pair, transform, 0)
    plane_ref[:, :8] = jnp.zeros((freqs, 8, 2 * WIDTH), F32)

    def spread_out(o, _):
        spec = spec_ref[o].reshape(slots, 2 * WIDTH).astype(BF)
        both = jnp.dot(spread_ref[o], spec, preferred_element_type=F32)
        half = freqs * pad_rows
        first = pl.multiple_of(o * tile_rows, 8)
        for k in range(freqs):
            by_re = both[k * pad_rows : (k + 1) * pad_rows]
            by_im = both[half + k * pad_rows : half + (k + 1) * pad_rows]
            here = jnp.concatenate(
                [by_re[:, :WIDTH] - by_im[:, WIDTH:], by_re[:, WIDTH:] + by_im[:, :WIDTH]], axis=1
            )
            plane_ref[k, pl.ds(first, 8)] += here[:8]
            plane_ref[k, pl.ds(first + 8, tile_rows)] = here[8:]
        return _

    lax.fori_loop(0, sky_count, spread_out, 0)

    def turn_rows(k, _):
        plane_ref[k, :8] += plane_ref[k, NX : NX + 8]
        plane = plane_ref[k, :NX].astype(BF)
        turned = lax.dot_general(
            plane, turn_ref[...], (((0,), (0,)), ((), ())), preferred_element_type=F32
        )
        out_ref[0, k] = turned[:WIDTH, :NX] + turned[WIDTH:, NX:]
        out_ref[1, k] = turned[WIDTH:, :NX] - turned[:WIDTH, NX:]
        return _

    lax.fori_loop(0, freqs, turn_rows, 0)


def shards(spectra, kernel, owner, offset):
    sky_count, gz_count = lax.axis_size("sky"), lax.axis_size("gz")
    slab = spectra.shape[1]
    tile_rows = NX // sky_count
    pad_rows = tile_rows + 8
    block, wide, per_row, cap = pack(spectra, kernel, owner, offset)
    slots = sky_count * cap
    got = gather(block, sky_count, gz_count)
    rest = got[:, slots : slots + (block.shape[0] - slots) // per_row * per_row].reshape(sky_count, gz_count, -1, per_row * wide)[:, :, :, :slots]
    narrow = slab - wide
    taps = KSIDE * KSIDE // gz_count
    tail = rest[:, :, :narrow].reshape(sky_count, gz_count * narrow, slots).transpose(0, 2, 1)

    def by_owner(item):
        item = item.reshape(-1, sky_count, cap).reshape(sky_count, -1, sky_count, cap)
        return item.transpose(2, 1, 0, 3).reshape(sky_count, -1, slots)

    weights = by_owner(rest[:, :, narrow : narrow + taps]).astype(F32)
    row = by_owner(rest[:, 0, narrow + taps])[:, 0].astype(jnp.int32)
    col = by_owner(rest[:, 0, narrow + taps + 1])[:, 0].astype(jnp.int32)

    per_block = NY // (sky_count * gz_count)
    first = (lax.axis_index("sky") * gz_count + lax.axis_index("gz")) * per_block
    freq = first + jnp.arange(per_block, dtype=jnp.int32)
    factor = 1.0 / math.sqrt(NY)
    side = [0.0] * KSIDE
    for b in range(KSIDE):
        phase = (freq[None, :, None] * (col + b)[:, None, :] % NY).astype(F32) * (2.0 * math.pi / NY)
        wave = jnp.stack([jnp.cos(phase), -jnp.sin(phase)], axis=1) * factor
        for a in range(KSIDE):
            side[a] = side[a] + wave * weights[:, None, None, a * KSIDE + b]
    lag = jnp.arange(pad_rows, dtype=jnp.int32)[None, :, None] - row[:, None, :]
    lag = lag[:, None, None]
    spread = jnp.zeros((), F32)
    for a in range(KSIDE):
        spread = jnp.where(lag == a, side[a][:, :, :, None, :], spread)
    spread = spread.astype(BF).reshape(sky_count, 2 * per_block * pad_rows, slots)

    chunks = -(-NW // WIDTH)
    cos_w, sin_w = dft_tables(NW)
    wave_table = np.zeros((NW, 2, chunks * WIDTH), np.float32)
    wave_table[:, 0, :NW], wave_table[:, 1, :NW] = cos_w, -sin_w
    wave_table = wave_table.reshape(gz_count, slab, 2, chunks, WIDTH)
    wave_table = np.concatenate(
        [
            wave_table[:, :wide].reshape(gz_count * wide, 2, chunks, WIDTH),
            wave_table[:, wide:].reshape(gz_count * narrow, 2, chunks, WIDTH),
        ]
    )
    wave_table = wave_table.transpose(2, 0, 1, 3).reshape(chunks, NW, 2 * WIDTH)
    turn = np.concatenate(dft_tables(NX), axis=1)

    dims = (sky_count, gz_count, cap, wide, tile_rows, pad_rows, per_block)
    macs = chunks * 2 * WIDTH * sky_count * slots * (NW + 2 * per_block * pad_rows)
    macs += chunks * 2 * WIDTH * 2 * NX * NX * per_block
    result = pl.pallas_call(
        functools.partial(cube_kernel, dims),
        grid=(chunks,),
        in_specs=[
            pl.BlockSpec(got.shape, lambda i: (0, 0, 0), pipeline_mode=pl.Buffered(1)),
            pl.BlockSpec(tail.shape, lambda i: (0, 0, 0), pipeline_mode=pl.Buffered(1)),
            pl.BlockSpec((1, NW, 2 * WIDTH), lambda i: (i, 0, 0)),
            pl.BlockSpec(spread.shape, lambda i: (0, 0, 0), pipeline_mode=pl.Buffered(1)),
            pl.BlockSpec(turn.shape, lambda i: (0, 0)),
        ],
        out_specs=pl.BlockSpec((2, per_block, WIDTH, NX), lambda i: (0, 0, i, 0)),
        out_shape=jax.ShapeDtypeStruct((2, per_block, NW, NX), F32),
        scratch_shapes=[
            pltpu.VMEM((sky_count, sky_count, cap, 2 * WIDTH), F32),
            pltpu.VMEM((per_block, NX + 8, 2 * WIDTH), F32),
        ],
        compiler_params=pltpu.CompilerParams(vmem_limit_bytes=56 * 1024 * 1024),
        cost_estimate=pl.CostEstimate(flops=2 * macs, bytes_accessed=32 * 1024 * 1024, transcendentals=0),
        interpret=INTERPRET,
    )(got, tail, jnp.asarray(wave_table, BF), spread, jnp.asarray(turn, BF))
    return result.transpose(0, 3, 1, 2)


def solution(mesh):
    in_specs = (P("sky", "gz"), P("sky", None), P("sky", None), P("sky"))
    out_specs = P(None, None, ("sky", "gz"), None)
    return jax.shard_map(shards, mesh=mesh, in_specs=in_specs, out_specs=out_specs, check_vma=False)
```
